32 devices in a mesh: gx: 8 (over z, x), gy: 2 (over y), gz: 2 (over core).
Axes of the slice: x: 2, y: 2, z: 4, core: 2. Of those that a mesh axis runs over, the one named last changes fastest.
Arguments:
- tokens: bfloat16 [2, 16, 4, 18432], P('gz', 'gy', None, 'gx'), may hold values from -40 to 40
- norm_gain: float32 [18432], P('gx'), may hold values from 0.2 to 1.8
- w_query: bfloat16 [18432, 12288], P('gx', 'gy'), may hold values from -0.046875 to 0.046875
- w_keyval: bfloat16 [18432, 512], P('gx', 'gy'), may hold values from -0.109375 to 0.109375
- cache_keys: bfloat16 [2, 16, 8192, 256], P('gz', ('gx', 'gy')), may hold values from -800 to 800
- cache_values: bfloat16 [2, 16, 8192, 256], P('gz', ('gx', 'gy')), may hold values from -6 to 6
- lengths: int32 [2, 16], P('gz', ('gx', 'gy')), may hold values from 1024 to 8192, as said below
Outputs:
- attended: bfloat16 [2, 16, 4, 12288], P('gz', ('gx', 'gy'))
- new_entries: bfloat16 [2, 16, 4, 512], P('gz', ('gx', 'gy'))
The draws below stay inside these ranges and needn't reach their ends.
Inputs may be any that keep to these rules, and one draw needn't show every extreme that they name: `lengths`: some sequence uses all 8192 positions.
All inputs are finite; a program needn't handle non-finite values.
Results may differ from the reference program's by a relative error of at most 0.02.
Values may be sent and summed in bfloat16 or wider, within the bound.
A program may use at most 64 MiB of HBM per device.

```python
import jax
import jax.numpy as jnp
from jax import lax

D = 18432
HEADS = 48
HD = 256
STEPS = 4
CACHE = 8192
SEQ_CORE = 16
N_GZ = 2


def draw_tokens(key, part):
    key = jax.random.fold_in(key, 11)
    column = jnp.arange(D, dtype=jnp.float32) / D
    baseline = jnp.clip(jax.random.normal(key, (N_GZ, SEQ_CORE, STEPS, D), jnp.float32), -6.0, 6.0)
    return (baseline * 3.0 ** column).astype(jnp.bfloat16)


def draw_cache_keys(key, part):
    key = jax.random.fold_in(key, 23)
    first_key = jax.random.fold_in(key, 0)
    baseline = jnp.clip(jax.random.normal(first_key, (N_GZ, SEQ_CORE, CACHE, HD), jnp.float32), -6.0, 6.0)
    return (2.0 * baseline).astype(jnp.bfloat16)


def draw_lengths(key, part):
    key = jax.random.fold_in(key, 37)
    first_key, second_key = jax.random.split(key)
    drawn = jax.random.randint(first_key, (N_GZ * SEQ_CORE,), CACHE // 8, CACHE + 1)
    chosen = jax.random.randint(second_key, (), 0, N_GZ * SEQ_CORE)
    drawn = jnp.where(jnp.arange(N_GZ * SEQ_CORE) == chosen, CACHE, drawn)
    return drawn.reshape(N_GZ, SEQ_CORE).astype(jnp.int32)


def shard_levels(own_key, dims, shards, smallest, top_value):
    def one(dim, shards_of):
        draws = jax.random.uniform(jax.random.fold_in(jax.random.fold_in(own_key, 6), dim), (shards_of,), jnp.float32, smallest / len(shards), top_value / len(shards))
        return jnp.repeat(jnp.exp(draws), dims[dim] // shards_of).reshape((-1,) + (1,) * (len(dims) - dim - 1))

    factor_of = one(*shards[0])
    for cut in shards[1:]:
        factor_of = factor_of * one(*cut)
    return factor_of


def noise(own_key, shape, scale, limit, cuts=(), kind=jnp.bfloat16):
    values = scale * jax.random.normal(own_key, shape, jnp.float32)
    if cuts:
        values = values * shard_levels(own_key, shape, cuts, -0.22, 0.18)
    return jnp.clip(values, -limit, limit).astype(kind)


def setup_inputs(seed: int = 0) -> dict:
    keys = jax.random.split(jax.random.key(seed), 8)
    tokens = draw_tokens(jax.random.fold_in(keys[7], 71), 0)
    norm_gain = jnp.clip(1.0 + 0.16 * jax.random.normal(keys[1], (D,), jnp.float32), 0.2, 1.8)
    w_query = noise(keys[2], (D, HEADS * HD), D ** -0.5, 0.046875, ((0, 8), (1, 2)))
    w_keyval = noise(keys[3], (D, 2 * HD), (D // 6) ** -0.5, 0.109375, ((0, 8), (1, 2)))
    cache_keys = draw_cache_keys(jax.random.fold_in(keys[7], 71), 0)
    cache_values = noise(keys[5], (N_GZ, SEQ_CORE, CACHE, HD), 1.0, 6.0, ((0, 2), (1, 16)))
    lengths = draw_lengths(jax.random.fold_in(keys[7], 71), 0)
    return dict(tokens=tokens, norm_gain=norm_gain, w_query=w_query, w_keyval=w_keyval, cache_keys=cache_keys, cache_values=cache_values, lengths=lengths)


def attend_one(entries):
    queries, keyvals, cache_key, cache_value, length = entries
    inverse_root = HD ** (-0.5)
    draft_keys = keyvals[:, :HD]
    draft_values = keyvals[:, HD:]
    cache_scores = jnp.dot(queries, cache_key.T, preferred_element_type=jnp.float32) * inverse_root
    draft_scores = jnp.dot(queries, draft_keys.T, preferred_element_type=jnp.float32) * inverse_root
    query_step = jnp.arange(STEPS * HEADS)[:, None] // HEADS
    draft_allowed = jnp.arange(STEPS)[None, :] <= query_step
    cache_allowed = (jnp.arange(CACHE) < length)[None, :]
    cache_scores = jnp.where(cache_allowed, cache_scores, -1e+30)
    draft_scores = jnp.where(draft_allowed, draft_scores, -1e+30)
    highest = jnp.maximum(lax.optimization_barrier(jnp.max(cache_scores, axis=-1)), lax.optimization_barrier(jnp.max(draft_scores, axis=-1)))
    cache_weights = jnp.where(cache_allowed, jnp.exp(cache_scores - highest[:, None]), 0.0)
    draft_weights = jnp.where(draft_allowed, jnp.exp(draft_scores - highest[:, None]), 0.0)
    denominator = lax.optimization_barrier(jnp.sum(cache_weights, axis=-1)) + lax.optimization_barrier(jnp.sum(draft_weights, axis=-1))
    summed = jnp.dot(cache_weights.astype(jnp.bfloat16), cache_value, preferred_element_type=jnp.float32)
    summed = summed + jnp.dot(draft_weights.astype(jnp.bfloat16), draft_values, preferred_element_type=jnp.float32)
    return (summed / denominator[:, None]).astype(jnp.bfloat16)

def reference(tokens, norm_gain, w_query, w_keyval, cache_keys, cache_values, lengths):
    values = tokens.astype(jnp.float32)
    center = lax.optimization_barrier(jnp.sum(values, axis=-1, keepdims=True)) / D
    spread = lax.optimization_barrier(jnp.sum(values * values, axis=-1, keepdims=True)) / D - center * center
    normed = ((values - center) * lax.rsqrt(spread + 1e-05) * norm_gain).astype(jnp.bfloat16)
    flat_rows = normed.reshape(N_GZ * SEQ_CORE * STEPS, D)
    queries = jnp.dot(flat_rows, w_query, preferred_element_type=jnp.float32).astype(jnp.bfloat16)
    keyvals = jnp.dot(flat_rows, w_keyval, preferred_element_type=jnp.float32).astype(jnp.bfloat16)
    queries = queries.reshape(N_GZ * SEQ_CORE, STEPS * HEADS, HD)
    keyvals = keyvals.reshape(N_GZ * SEQ_CORE, STEPS, 2 * HD)
    attended = lax.map(attend_one, (queries, keyvals, cache_keys.reshape(N_GZ * SEQ_CORE, CACHE, HD), cache_values.reshape(N_GZ * SEQ_CORE, CACHE, HD), lengths.reshape(N_GZ * SEQ_CORE)))
    return (attended.reshape(N_GZ, SEQ_CORE, STEPS, HEADS * HD), keyvals.reshape(N_GZ, SEQ_CORE, STEPS, 2 * HD))
```

```python
import functools
import math

import jax
import jax.numpy as jnp
from jax import lax
from jax.experimental import pallas as pl
from jax.experimental.pallas import tpu as pltpu
from jax.sharding import PartitionSpec as P

D = 18432
HD = 256
OUTER = 4
LANES = 128
PACK = 16
MESH = pl.DeviceIdType.MESH


def project_kernel(
    sizes,
    x_ref,
    gain_ref,
    wq_hbm,
    wkv_hbm,
    out_ref,
    wq,
    wkv,
    rows,
    stat_send,
    stat_recv,
    product,
    a_send,
    a_recv,
    kept,
    b_send,
    b_recv,
    own,
    c_send,
    c_recv,
    w_sem,
    st_ssem,
    st_rsem,
    y_ssem,
    y_rsem,
    k_ssem,
    k_rsem,
    a_ssem,
    a_rsem,
    b_ssem,
    b_rsem,
    c_ssem,
    c_rsem,
):
    X, Y, Z, seqs, steps = sizes
    NZ = OUTER
    NX = X // NZ
    G = Y * Z
    block = seqs * steps
    group = Y * steps
    per_block = seqs // Y
    dest_rows = Z * group
    query_half = wq.shape[1]
    keyval_half = wkv.shape[1]
    width = a_send.shape[-1]
    query_chunks = query_half // width
    chunks = query_chunks + 1

    i = lax.axis_index("gx")
    j = lax.axis_index("gy")
    k = lax.axis_index("gz")
    zi = i // NX
    xi = i % NX
    me = j * Z + k

    def chunk_width(c):
        return width if c < query_chunks else keyval_half

    def query_load(c):
        begin = pl.multiple_of(k * query_half + c * width, LANES)
        return pltpu.make_async_copy(
            wq_hbm.at[:, pl.ds(begin, width)],
            wq.at[:, pl.ds(c * width, width)],
            w_sem.at[c],
        )

    keyval_load = pltpu.make_async_copy(
        wkv_hbm.at[:, pl.ds(pl.multiple_of(k * keyval_half, LANES), keyval_half)],
        wkv,
        w_sem.at[query_chunks],
    )
    loads = [query_load(c) for c in range(query_chunks)] + [keyval_load]
    for load in loads:
        load.start()

    barrier = pltpu.get_barrier_semaphore()
    for d in range(1, X):
        pl.semaphore_signal(
            barrier, inc=1, device_id={"gx": (i + d) % X, "gy": j, "gz": k}, device_id_type=MESH
        )
    for dj in range(Y):
        for dk in range(Z):
            if dj or dk:
                pl.semaphore_signal(
                    barrier,
                    inc=1,
                    device_id={"gx": i, "gy": (j + dj) % Y, "gz": (k + dk) % Z},
                    device_id_type=MESH,
                )

    values = x_ref[...].astype(jnp.float32)
    row_sum = jnp.sum(values, axis=1, keepdims=True)
    row_square = jnp.sum(values * values, axis=1, keepdims=True)
    lane = lax.broadcasted_iota(jnp.int32, (block, LANES), 1)
    packed = jnp.where(lane == 0, row_sum, jnp.where(lane == 1, row_square, 0.0))
    packed = jnp.concatenate(
        (packed, jnp.zeros((LANES - block, LANES), jnp.float32)), axis=0
    )
    stat_send[...] = packed.T[:8]

    pl.semaphore_wait(barrier, X - 1 + G - 1)

    sends = []

    def send(src, dst, ssem, rsem, di, dj, dk):
        copy = pltpu.make_async_remote_copy(
            src_ref=src,
            dst_ref=dst,
            send_sem=ssem,
            recv_sem=rsem,
            device_id={"gx": di, "gy": dj, "gz": dk},
            device_id_type=MESH,
        )
        copy.start()
        sends.append(copy)
        return copy

    stat_copies = [
        send(stat_send, stat_recv.at[d], st_ssem.at[d], st_rsem.at[d], (i + d) % X, j, k)
        for d in range(1, X)
    ]
    total = stat_send[...]
    for d in range(1, X):
        stat_copies[d - 1].wait_recv()
        total = total + stat_recv[d]
    total = jnp.concatenate((total, jnp.zeros((LANES - 8, LANES), jnp.float32)), axis=0).T
    center = total[:block, 0:1] / D
    spread = total[:block, 1:2] / D - center * center
    factor = lax.rsqrt(spread + 1e-05)
    normed = ((x_ref[...].astype(jnp.float32) - center) * factor * gain_ref[...]).astype(jnp.bfloat16)
    own_rows = pl.ds(pl.multiple_of(me * block, block), block)
    rows[own_rows, :] = normed

    def row_block(dj):
        g = ((j + Y - dj) % Y) * Z + k
        return rows.at[pl.ds(pl.multiple_of(g * block, block), block), :]

    y_copies = [None] + [
        send(row_block(0), row_block(0), y_ssem.at[dj], y_rsem.at[dj], i, (j + dj) % Y, k)
        for dj in range(1, Y)
    ]
    k_copies = []
    for dj in range(Y):
        if dj:
            y_copies[dj].wait_recv()
        for dk in range(1, Z):
            k_copies.append(
                send(
                    row_block(dj),
                    row_block(dj),
                    k_ssem.at[dj, dk],
                    k_rsem.at[dj, dk],
                    i,
                    j,
                    (k + dk) % Z,
                )
            )
    for copy in k_copies:
        copy.wait_recv()

    def multiply(c):
        loads[c].wait()
        if c < query_chunks:
            tile = HD

            def body(n, carry):
                here = pl.ds(pl.multiple_of(n * tile, tile), tile)
                there = pl.ds(pl.multiple_of(c * width + n * tile, tile), tile)
                product[:, here] = jnp.dot(
                    rows[...], wq[:, there], preferred_element_type=jnp.float32
                )
                return carry

            lax.fori_loop(0, width // tile, body, 0)
        else:
            product[:, :keyval_half] = jnp.dot(
                rows[...], wkv[...], preferred_element_type=jnp.float32
            )

    def rows_for(di, dk, w):
        g = (di // per_block) * Z + dk
        begin = pl.multiple_of(g * block + (di % per_block) * group, group)
        return product[pl.ds(begin, group), :w]

    a_copies = {}
    b_copies = {}
    c_copies = {}

    def stage_a(c):
        w = chunk_width(c)
        for dx in range(1, NX):
            to_x = (xi + dx) % NX
            for z in range(NZ):
                part = jnp.concatenate(
                    [rows_for(z * NX + to_x, dk, w) for dk in range(Z)], axis=0
                )
                a_send[c, dx, z * dest_rows : (z + 1) * dest_rows, :w] = part.astype(jnp.bfloat16)
            a_copies[c, dx] = send(
                a_send.at[c, dx, :, :w],
                a_recv.at[c, dx, :, :w],
                a_ssem.at[c, dx],
                a_rsem.at[c, dx],
                zi * NX + to_x,
                j,
                k,
            )
        for z in range(NZ):
            kept[c, z, :, :w] = jnp.concatenate(
                [rows_for(z * NX + xi, dk, w) for dk in range(Z)], axis=0
            )

    def stage_b(c):
        w = chunk_width(c)
        for dx in range(1, NX):
            a_copies[c, dx].wait_recv()
        for z in range(NZ):
            part = kept[c, z, :, :w]
            for dx in range(1, NX):
                part = part + a_recv[
                    c, dx, z * dest_rows : (z + 1) * dest_rows, :w
                ].astype(jnp.float32)
            kept[c, z, :, :w] = part
            b_send[c, z, :, :w] = part.astype(jnp.bfloat16)
        for dz in range(1, NZ):
            to_z = (zi + dz) % NZ
            b_copies[c, dz] = send(
                b_send.at[c, to_z, :, :w],
                b_recv.at[c, dz, :, :w],
                b_ssem.at[c, dz],
                b_rsem.at[c, dz],
                to_z * NX + xi,
                j,
                k,
            )
        own[c, :, :w] = kept[c, zi, :, :w]

    def stage_c(c):
        w = chunk_width(c)
        part = own[c, :, :w]
        for dz in range(1, NZ):
            b_copies[c, dz].wait_recv()
            part = part + b_recv[c, dz, :, :w].astype(jnp.float32)
        for dj in range(Y):
            for dk in range(Z):
                begin = (dk * Y + dj) * steps
                mine = part[begin : begin + steps, :]
                if w < HD:
                    mine = jnp.concatenate(
                        (mine, jnp.zeros((steps, HD - w), jnp.float32)), axis=1
                    )
                pieces = [mine[:, h * HD : (h + 1) * HD] for h in range(mine.shape[1] // HD)]
                missing = PACK - steps * len(pieces)
                if missing:
                    pieces.append(jnp.zeros((missing, HD), jnp.float32))
                c_send[c, dj * Z + dk] = jnp.concatenate(pieces, axis=0).astype(jnp.bfloat16)
        for dj in range(Y):
            for dk in range(Z):
                if dj or dk:
                    to_j = (j + dj) % Y
                    to_k = (k + dk) % Z
                    slot = dj * Z + dk
                    c_copies[c, slot] = send(
                        c_send.at[c, to_j * Z + to_k],
                        c_recv.at[c, me],
                        c_ssem.at[c, slot],
                        c_rsem.at[c, slot],
                        i,
                        to_j,
                        to_k,
                    )
        c_recv[c, me] = c_send[c, me]

    for c in range(chunks + 2):
        if c < chunks:
            multiply(c)
            stage_a(c)
        if 1 <= c < chunks + 1:
            stage_b(c - 1)
        if 2 <= c:
            stage_c(c - 2)
    for copy in c_copies.values():
        copy.wait_recv()
    out_ref[...] = c_recv[...]
    for copy in sends:
        copy.wait_send()


def project(tokens, gain, w_query, w_keyval):
    X, Y, Z = lax.axis_size("gx"), lax.axis_size("gy"), lax.axis_size("gz")
    seqs, steps, depth = tokens.shape
    G = Y * Z
    NZ = OUTER
    NX = X // NZ
    block = seqs * steps
    dest_rows = Z * Y * steps
    query_half = w_query.shape[1] // Z
    keyval_half = w_keyval.shape[1] // Z
    width = min(query_half, HD * (PACK // steps))
    chunks = query_half // width + 1
    bf16, f32 = jnp.bfloat16, jnp.float32
    any_space = pl.BlockSpec(memory_space=pl.ANY)
    vmem = pl.BlockSpec(memory_space=pltpu.VMEM)
    dma = pltpu.SemaphoreType.DMA
    return pl.pallas_call(
        functools.partial(project_kernel, (X, Y, Z, seqs, steps)),
        out_shape=jax.ShapeDtypeStruct((chunks, G, PACK, HD), bf16),
        in_specs=[vmem, vmem, any_space, any_space],
        out_specs=vmem,
        scratch_shapes=[
            pltpu.VMEM((depth, query_half), bf16),
            pltpu.VMEM((depth, keyval_half), bf16),
            pltpu.VMEM((G * block, depth), bf16),
            pltpu.VMEM((8, LANES), f32),
            pltpu.VMEM((X, 8, LANES), f32),
            pltpu.VMEM((G * block, width), f32),
            pltpu.VMEM((chunks, NX, NZ * dest_rows, width), bf16),
            pltpu.VMEM((chunks, NX, NZ * dest_rows, width), bf16),
            pltpu.VMEM((chunks, NZ, dest_rows, width), f32),
            pltpu.VMEM((chunks, NZ, dest_rows, width), bf16),
            pltpu.VMEM((chunks, NZ, dest_rows, width), bf16),
            pltpu.VMEM((chunks, dest_rows, width), f32),
            pltpu.VMEM((chunks, G, PACK, HD), bf16),
            pltpu.VMEM((chunks, G, PACK, HD), bf16),
            dma((chunks,)),
            dma((X,)),
            dma((X,)),
            dma((Y,)),
            dma((Y,)),
            dma((Y, Z)),
            dma((Y, Z)),
            dma((chunks, NX)),
            dma((chunks, NX)),
            dma((chunks, NZ)),
            dma((chunks, NZ)),
            dma((chunks, G)),
            dma((chunks, G)),
        ],
        compiler_params=pltpu.CompilerParams(
            collective_id=0, has_side_effects=True, vmem_limit_bytes=56 * 2**20
        ),
        cost_estimate=pl.CostEstimate(
            flops=2 * G * block * depth * (query_half + keyval_half),
            bytes_accessed=2 * depth * (query_half + keyval_half),
            transcendentals=0,
        ),
    )(tokens.reshape(block, depth), gain.reshape(1, depth), w_query, w_keyval)


def attend_kernel(sizes, len_ref, q_ref, k_ref, v_ref, out_ref, new_ref, acc, top, total):
    heads, steps, keyval_real = sizes
    chunks, G = q_ref.shape[0] - 1, q_ref.shape[1]
    query_rows = chunks * G * PACK
    scale = HD**-0.5 * math.log2(math.e)
    p = pl.program_id(0)
    span = k_ref.shape[0]
    queries = q_ref[:chunks].reshape(query_rows, HD)
    transposed = (((1,), (1,)), ((), ()))

    @pl.when(p == 0)
    def _():
        entries = jnp.concatenate(
            [q_ref[chunks, g, :, :keyval_real] for g in range(G)], axis=1
        )
        new_ref[...] = entries[:steps]
        scores = scale * lax.dot_general(
            queries, entries[:, :HD], transposed, preferred_element_type=jnp.float32
        )
        row_step = lax.broadcasted_iota(jnp.int32, scores.shape, 0) % steps
        entry_step = lax.broadcasted_iota(jnp.int32, scores.shape, 1)
        scores = jnp.where(entry_step <= row_step, scores, -1e30)
        highest = jnp.max(scores, axis=1, keepdims=True)
        weights = jnp.exp2(scores - highest)
        top[...] = jnp.broadcast_to(highest, top.shape)
        total[...] = jnp.broadcast_to(jnp.sum(weights, axis=1, keepdims=True), total.shape)
        acc[...] = jnp.dot(
            weights.astype(jnp.bfloat16), entries[:, HD:], preferred_element_type=jnp.float32
        )

    scores = scale * lax.dot_general(
        queries, k_ref[...], transposed, preferred_element_type=jnp.float32
    )
    position = p * span + lax.broadcasted_iota(jnp.int32, (1, span), 1)
    scores = jnp.where(position < len_ref[0, 0], scores, -1e30)
    before = top[:, :1]
    highest = jnp.maximum(before, jnp.max(scores, axis=1, keepdims=True))
    weights = jnp.exp2(scores - highest)
    keep = jnp.exp2(before - highest)
    top[...] = jnp.broadcast_to(highest, top.shape)
    total[...] = total[...] * keep + jnp.sum(weights, axis=1, keepdims=True)
    acc[...] = acc[...] * keep + jnp.dot(
        weights.astype(jnp.bfloat16), v_ref[...], preferred_element_type=jnp.float32
    )

    @pl.when(p == pl.num_programs(0) - 1)
    def _():
        result = acc[...] / total[:, :1]
        per_group = heads // G
        per_chunk = per_group // chunks
        for c in range(chunks):
            for g in range(G):
                for h in range(per_chunk):
                    begin = (c * G + g) * PACK + h * steps
                    head = g * per_group + c * per_chunk + h
                    out_ref[:, head * HD : (head + 1) * HD] = result[
                        begin : begin + steps
                    ].astype(jnp.bfloat16)


def attend(packed, cache_keys, cache_values, lengths, heads, steps, keyval_real):
    chunks, G = packed.shape[0] - 1, packed.shape[1]
    query_rows = chunks * G * PACK
    cache_len = cache_keys.shape[0]
    span = 1024
    whole = pl.BlockSpec(packed.shape, lambda p: (0, 0, 0, 0))
    return pl.pallas_call(
        functools.partial(attend_kernel, (heads, steps, keyval_real)),
        grid=(cache_len // span,),
        out_shape=(
            jax.ShapeDtypeStruct((steps, heads * HD), jnp.bfloat16),
            jax.ShapeDtypeStruct((steps, 2 * HD), jnp.bfloat16),
        ),
        in_specs=[
            pl.BlockSpec(memory_space=pltpu.SMEM),
            whole,
            pl.BlockSpec((span, HD), lambda p: (p, 0)),
            pl.BlockSpec((span, HD), lambda p: (p, 0)),
        ],
        out_specs=(
            pl.BlockSpec((steps, heads * HD), lambda p: (0, 0)),
            pl.BlockSpec((steps, 2 * HD), lambda p: (0, 0)),
        ),
        scratch_shapes=[
            pltpu.VMEM((query_rows, HD), jnp.float32),
            pltpu.VMEM((query_rows, LANES), jnp.float32),
            pltpu.VMEM((query_rows, LANES), jnp.float32),
        ],
        compiler_params=pltpu.CompilerParams(vmem_limit_bytes=32 * 2**20),
        cost_estimate=pl.CostEstimate(
            flops=4 * query_rows * cache_len * HD,
            bytes_accessed=4 * cache_len * HD,
            transcendentals=query_rows * cache_len,
        ),
    )(lengths, packed, cache_keys, cache_values)


def on_device(tokens, norm_gain, w_query, w_keyval, cache_keys, cache_values, lengths):
    inputs = tokens[0]
    steps = inputs.shape[1]
    Y, Z = lax.axis_size("gy"), lax.axis_size("gz")
    heads = w_query.shape[1] * Y // HD
    keyval_real = w_keyval.shape[1] // Z
    missing = -keyval_real % LANES
    if missing:
        split = w_keyval.reshape(w_keyval.shape[0], Z, keyval_real)
        w_keyval = jnp.pad(split, ((0, 0), (0, 0), (0, missing))).reshape(w_keyval.shape[0], -1)
    packed = project(inputs, norm_gain, w_query, w_keyval)
    attended, entries = attend(
        packed, cache_keys[0, 0], cache_values[0, 0], lengths, heads, steps, keyval_real
    )
    return (attended[None, None], entries[None, None])


def solution(mesh):
    return jax.shard_map(
        on_device,
        mesh=mesh,
        in_specs=(
            P("gz", "gy", None, "gx"),
            P("gx"),
            P("gx", "gy"),
            P("gx", "gy"),
            P("gz", ("gx", "gy"), None, None),
            P("gz", ("gx", "gy"), None, None),
            P("gz", ("gx", "gy")),
        ),
        out_specs=(P("gz", ("gx", "gy"), None, None), P("gz", ("gx", "gy"), None, None)),
        check_vma=False,
    )
```

```python
import functools
import math

import jax
import jax.numpy as jnp
from jax import lax
from jax.experimental import pallas as pl
from jax.experimental.pallas import tpu as pltpu
from jax.sharding import PartitionSpec as P

D = 18432
HD = 256
OUTER = 4
LANES = 128
PACK = 16
AHEAD = 2
WIDTH = 512
MESH = pl.DeviceIdType.MESH


def project_kernel(
    sizes,
    x_ref,
    gain_ref,
    wq_hbm,
    wkv_hbm,
    out_ref,
    wq,
    wkv,
    raw,
    rows,
    stat_send,
    stat_recv,
    scale_send,
    scale_recv,
    product,
    a_send,
    a_recv,
    kept,
    b_send,
    b_recv,
    own,
    c_send,
    c_recv,
    w_sem,
    st_ssem,
    st_rsem,
    sc_ssem,
    sc_rsem,
    y_ssem,
    y_rsem,
    k_ssem,
    k_rsem,
    a_ssem,
    a_rsem,
    b_ssem,
    b_rsem,
    c_ssem,
    c_rsem,
):
    X, Y, Z, seqs, steps = sizes
    NZ = OUTER
    NX = X // NZ
    G = Y * Z
    block = seqs * steps
    group = Y * steps
    per_block = seqs // Y
    dest_rows = Z * group
    query_half = wq.shape[1]
    keyval_half = wkv.shape[1]
    width = a_send.shape[-1]
    query_chunks = query_half // width
    chunks = query_chunks + 1
    packs = c_send.shape[0]
    subs = query_chunks // (packs - 1)

    i = lax.axis_index("gx")
    j = lax.axis_index("gy")
    k = lax.axis_index("gz")
    zi = i // NX
    xi = i % NX
    me = j * Z + k

    def chunk_width(c):
        return width if c < query_chunks else keyval_half

    def query_load(c):
        begin = pl.multiple_of(k * query_half + c * width, LANES)
        return pltpu.make_async_copy(
            wq_hbm.at[:, pl.ds(begin, width)],
            wq.at[:, pl.ds(c * width, width)],
            w_sem.at[c],
        )

    keyval_load = pltpu.make_async_copy(
        wkv_hbm.at[:, pl.ds(pl.multiple_of(k * keyval_half, LANES), keyval_half)],
        wkv,
        w_sem.at[query_chunks],
    )
    loads = [query_load(c) for c in range(query_chunks)] + [keyval_load]
    for load in loads:
        load.start()

    barrier = pltpu.get_barrier_semaphore()
    for d in range(1, X):
        pl.semaphore_signal(
            barrier, inc=1, device_id={"gx": (i + d) % X, "gy": j, "gz": k}, device_id_type=MESH
        )
    for dj in range(Y):
        for dk in range(Z):
            if dj or dk:
                pl.semaphore_signal(
                    barrier,
                    inc=1,
                    device_id={"gx": i, "gy": (j + dj) % Y, "gz": (k + dk) % Z},
                    device_id_type=MESH,
                )

    values = jnp.concatenate(
        [x_ref[0, q].astype(jnp.float32) for q in range(seqs)], axis=0
    )

    def row_range(dj, dk):
        g = ((j + Y - dj) % Y) * Z + (k + Z - dk) % Z
        return pl.ds(pl.multiple_of(g * block, block), block)

    raw[row_range(0, 0), :] = values.astype(jnp.bfloat16)
    row_sum = jnp.sum(values, axis=1, keepdims=True)
    row_square = jnp.sum(values * values, axis=1, keepdims=True)
    lane = lax.broadcasted_iota(jnp.int32, (block, LANES), 1)
    packed = jnp.where(lane == 0, row_sum, jnp.where(lane == 1, row_square, 0.0))
    packed = jnp.concatenate(
        (packed, jnp.zeros((LANES - block, LANES), jnp.float32)), axis=0
    )
    stat_send[...] = packed.T[:8]

    pl.semaphore_wait(barrier, X - 1 + G - 1)

    sends = []

    def send(src, dst, ssem, rsem, di, dj, dk):
        copy = pltpu.make_async_remote_copy(
            src_ref=src,
            dst_ref=dst,
            send_sem=ssem,
            recv_sem=rsem,
            device_id={"gx": di, "gy": dj, "gz": dk},
            device_id_type=MESH,
        )
        copy.start()
        sends.append(copy)
        return copy

    stat_copies = [
        send(stat_send, stat_recv.at[d], st_ssem.at[d], st_rsem.at[d], (i + d) % X, j, k)
        for d in range(1, X)
    ]

    def raw_block(dj):
        return raw.at[row_range(dj, 0), :]

    y_copies = [None] + [
        send(raw_block(0), raw_block(0), y_ssem.at[dj], y_rsem.at[dj], i, (j + dj) % Y, k)
        for dj in range(1, Y)
    ]
    k_copies = {}

    def pass_on(dj):
        for dk in range(1, Z):
            k_copies[dj, dk] = send(
                raw_block(dj),
                raw_block(dj),
                k_ssem.at[dj, dk],
                k_rsem.at[dj, dk],
                i,
                j,
                (k + dk) % Z,
            )

    pass_on(0)
    total = stat_send[...]
    for d in range(1, X):
        stat_copies[d - 1].wait_recv()
        total = total + stat_recv[d]
    center = total[0:1] / D
    spread = total[1:2] / D - center * center
    scale_send[...] = jnp.concatenate(
        (center, lax.rsqrt(spread + 1e-05), jnp.zeros((6, LANES), jnp.float32)), axis=0
    )
    scale_copies = {}
    for dj in range(Y):
        for dk in range(Z):
            if dj or dk:
                slot = dj * Z + dk
                scale_copies[slot] = send(
                    scale_send,
                    scale_recv.at[slot],
                    sc_ssem.at[slot],
                    sc_rsem.at[slot],
                    i,
                    (j + dj) % Y,
                    (k + dk) % Z,
                )
    for dj in range(1, Y):
        y_copies[dj].wait_recv()
        pass_on(dj)
    for copy in scale_copies.values():
        copy.wait_recv()
    scales = [scale_send[...]] + [scale_recv[slot] for slot in range(1, G)]
    if 8 * G < LANES:
        scales.append(jnp.zeros((LANES - 8 * G, LANES), jnp.float32))
    scales = jnp.concatenate(scales, axis=0).T
    gain = gain_ref[...].reshape(1, gain_ref.shape[0])
    for dk in range(Z):
        for dj in range(Y):
            if dk:
                k_copies[dj, dk].wait_recv()
            here = row_range(dj, dk)
            slot = dj * Z + dk
            center = scales[:block, 8 * slot : 8 * slot + 1]
            factor = scales[:block, 8 * slot + 1 : 8 * slot + 2]
            rows[here, :] = (
                (raw[here, :].astype(jnp.float32) - center) * factor * gain
            ).astype(jnp.bfloat16)

    def multiply(c):
        loads[c].wait()
        if c < query_chunks:
            tile = HD

            def body(n, carry):
                here = pl.ds(pl.multiple_of(n * tile, tile), tile)
                there = pl.ds(pl.multiple_of(c * width + n * tile, tile), tile)
                product[:, here] = jnp.dot(
                    rows[...], wq[:, there], preferred_element_type=jnp.float32
                )
                return carry

            lax.fori_loop(0, width // tile, body, 0)
        else:
            product[:, :keyval_half] = jnp.dot(
                rows[...], wkv[...], preferred_element_type=jnp.float32
            )

    def rows_for(di, dk, w):
        g = (di // per_block) * Z + dk
        begin = pl.multiple_of(g * block + (di % per_block) * group, group)
        return product[pl.ds(begin, group), :w]

    a_copies = {}
    b_copies = {}
    c_copies = {}

    def stage_a(c):
        w = chunk_width(c)
        for dx in range(1, NX):
            to_x = (xi + dx) % NX
            for z in range(NZ):
                part = jnp.concatenate(
                    [rows_for(z * NX + to_x, dk, w) for dk in range(Z)], axis=0
                )
                a_send[c, dx, z * dest_rows : (z + 1) * dest_rows, :w] = part.astype(jnp.bfloat16)
            a_copies[c, dx] = send(
                a_send.at[c, dx, :, :w],
                a_recv.at[c, dx, :, :w],
                a_ssem.at[c, dx],
                a_rsem.at[c, dx],
                zi * NX + to_x,
                j,
                k,
            )
        for z in range(NZ):
            kept[c, z, :, :w] = jnp.concatenate(
                [rows_for(z * NX + xi, dk, w) for dk in range(Z)], axis=0
            )

    def stage_b(c):
        w = chunk_width(c)
        for dx in range(1, NX):
            a_copies[c, dx].wait_recv()
        for z in range(NZ):
            part = kept[c, z, :, :w]
            for dx in range(1, NX):
                part = part + a_recv[
                    c, dx, z * dest_rows : (z + 1) * dest_rows, :w
                ].astype(jnp.float32)
            kept[c, z, :, :w] = part
            b_send[c, z, :, :w] = part.astype(jnp.bfloat16)
        for dz in range(1, NZ):
            to_z = (zi + dz) % NZ
            b_copies[c, dz] = send(
                b_send.at[c, to_z, :, :w],
                b_recv.at[c, dz, :, :w],
                b_ssem.at[c, dz],
                b_rsem.at[c, dz],
                to_z * NX + xi,
                j,
                k,
            )
        own[c, :, :w] = kept[c, zi, :, :w]

    def stage_c(c):
        members = range(c * subs, (c + 1) * subs) if c < packs - 1 else [query_chunks]
        parts = []
        for m in members:
            w = chunk_width(m)
            part = own[m, :, :w]
            for dz in range(1, NZ):
                b_copies[m, dz].wait_recv()
                part = part + b_recv[m, dz, :, :w].astype(jnp.float32)
            parts.append(part)
        part = jnp.concatenate(parts, axis=1)
        w = part.shape[1]
        for dj in range(Y):
            for dk in range(Z):
                begin = (dk * Y + dj) * steps
                mine = part[begin : begin + steps, :]
                if w < HD:
                    mine = jnp.concatenate(
                        (mine, jnp.zeros((steps, HD - w), jnp.float32)), axis=1
                    )
                pieces = [mine[:, h * HD : (h + 1) * HD] for h in range(mine.shape[1] // HD)]
                missing = PACK - steps * len(pieces)
                if missing:
                    pieces.append(jnp.zeros((missing, HD), jnp.float32))
                c_send[c, dj * Z + dk] = jnp.concatenate(pieces, axis=0).astype(jnp.bfloat16)
        for dj in range(Y):
            for dk in range(Z):
                if dj or dk:
                    to_j = (j + dj) % Y
                    to_k = (k + dk) % Z
                    slot = dj * Z + dk
                    c_copies[c, slot] = send(
                        c_send.at[c, to_j * Z + to_k],
                        c_recv.at[c, me],
                        c_ssem.at[c, slot],
                        c_rsem.at[c, slot],
                        i,
                        to_j,
                        to_k,
                    )
        c_recv[c, me] = c_send[c, me]

    done = 0
    for c in range(chunks + AHEAD):
        if c < chunks:
            multiply(c)
            stage_a(c)
        if c >= AHEAD:
            stage_b(c - AHEAD)
            if done < packs - 1 and c - AHEAD >= (done + 1) * subs + 1:
                stage_c(done)
                done += 1
    for c in range(done, packs):
        stage_c(c)
    for copy in c_copies.values():
        copy.wait_recv()
    out_ref[...] = c_recv[...]
    for copy in sends:
        copy.wait_send()


def project(tokens, gain, w_query, w_keyval):
    X, Y, Z = lax.axis_size("gx"), lax.axis_size("gy"), lax.axis_size("gz")
    seqs, steps, depth = tokens.shape[1:]
    G = Y * Z
    NZ = OUTER
    NX = X // NZ
    block = seqs * steps
    dest_rows = Z * Y * steps
    query_half = w_query.shape[1] // Z
    keyval_half = w_keyval.shape[1] // Z
    pack_width = min(query_half, HD * (PACK // steps))
    width = WIDTH if pack_width % WIDTH == 0 else pack_width
    chunks = query_half // width + 1
    packs = query_half // pack_width + 1
    bf16, f32 = jnp.bfloat16, jnp.float32
    any_space = pl.BlockSpec(memory_space=pl.ANY)
    vmem = pl.BlockSpec(memory_space=pltpu.VMEM)
    dma = pltpu.SemaphoreType.DMA
    return pl.pallas_call(
        functools.partial(project_kernel, (X, Y, Z, seqs, steps)),
        out_shape=jax.ShapeDtypeStruct((packs, G, PACK, HD), bf16),
        in_specs=[vmem, vmem, any_space, any_space],
        out_specs=vmem,
        scratch_shapes=[
            pltpu.VMEM((depth, query_half), bf16),
            pltpu.VMEM((depth, keyval_half), bf16),
            pltpu.VMEM((G * block, depth), bf16),
            pltpu.VMEM((G * block, depth), bf16),
            pltpu.VMEM((8, LANES), f32),
            pltpu.VMEM((X, 8, LANES), f32),
            pltpu.VMEM((8, LANES), f32),
            pltpu.VMEM((G, 8, LANES), f32),
            pltpu.VMEM((G * block, width), f32),
            pltpu.VMEM((chunks, NX, NZ * dest_rows, width), bf16),
            pltpu.VMEM((chunks, NX, NZ * dest_rows, width), bf16),
            pltpu.VMEM((chunks, NZ, dest_rows, width), f32),
            pltpu.VMEM((chunks, NZ, dest_rows, width), bf16),
            pltpu.VMEM((chunks, NZ, dest_rows, width), bf16),
            pltpu.VMEM((chunks, dest_rows, width), f32),
            pltpu.VMEM((packs, G, PACK, HD), bf16),
            pltpu.VMEM((packs, G, PACK, HD), bf16),
            dma((chunks,)),
            dma((X,)),
            dma((X,)),
            dma((G,)),
            dma((G,)),
            dma((Y,)),
            dma((Y,)),
            dma((Y, Z)),
            dma((Y, Z)),
            dma((chunks, NX)),
            dma((chunks, NX)),
            dma((chunks, NZ)),
            dma((chunks, NZ)),
            dma((packs, G)),
            dma((packs, G)),
        ],
        compiler_params=pltpu.CompilerParams(
            collective_id=0, has_side_effects=True, vmem_limit_bytes=32 * 2**20
        ),
        cost_estimate=pl.CostEstimate(
            flops=2 * G * block * depth * (query_half + keyval_half),
            bytes_accessed=2 * depth * (query_half + keyval_half),
            transcendentals=0,
        ),
    )(tokens, gain, w_query, w_keyval)


def attend_kernel(sizes, len_ref, q_ref, k_ref, v_ref, out_ref, new_ref, acc, top, total):
    heads, steps, keyval_real = sizes
    chunks, G = q_ref.shape[0] - 1, q_ref.shape[1]
    query_rows = chunks * G * PACK
    scale = HD**-0.5 * math.log2(math.e)
    p = pl.program_id(0)
    span = k_ref.shape[0]
    queries = q_ref[:chunks].reshape(query_rows, HD)
    transposed = (((1,), (1,)), ((), ()))

    @pl.when(p == 0)
    def _():
        entries = jnp.concatenate(
            [q_ref[chunks, g, :, :keyval_real] for g in range(G)], axis=1
        )
        new_ref[...] = entries[:steps]
        scores = scale * lax.dot_general(
            queries, entries[:, :HD], transposed, preferred_element_type=jnp.float32
        )
        row_step = lax.broadcasted_iota(jnp.int32, scores.shape, 0) % steps
        entry_step = lax.broadcasted_iota(jnp.int32, scores.shape, 1)
        scores = jnp.where(entry_step <= row_step, scores, -1e30)
        highest = jnp.max(scores, axis=1, keepdims=True)
        weights = jnp.exp2(scores - highest)
        top[...] = jnp.broadcast_to(highest, top.shape)
        total[...] = jnp.broadcast_to(jnp.sum(weights, axis=1, keepdims=True), total.shape)
        acc[...] = jnp.dot(
            weights.astype(jnp.bfloat16), entries[:, HD:], preferred_element_type=jnp.float32
        )

    scores = scale * lax.dot_general(
        queries, k_ref[...], transposed, preferred_element_type=jnp.float32
    )
    position = p * span + lax.broadcasted_iota(jnp.int32, (1, span), 1)
    scores = jnp.where(position < len_ref[0, 0], scores, -1e30)
    before = top[:, :1]
    highest = jnp.maximum(before, jnp.max(scores, axis=1, keepdims=True))
    weights = jnp.exp2(scores - highest)
    keep = jnp.exp2(before - highest)
    top[...] = jnp.broadcast_to(highest, top.shape)
    total[...] = total[...] * keep + jnp.sum(weights, axis=1, keepdims=True)
    acc[...] = acc[...] * keep + jnp.dot(
        weights.astype(jnp.bfloat16), v_ref[...], preferred_element_type=jnp.float32
    )

    @pl.when(p == pl.num_programs(0) - 1)
    def _():
        result = acc[...] / total[:, :1]
        per_group = heads // G
        per_chunk = per_group // chunks
        for c in range(chunks):
            for g in range(G):
                for h in range(per_chunk):
                    begin = (c * G + g) * PACK + h * steps
                    head = g * per_group + c * per_chunk + h
                    out_ref[:, head * HD : (head + 1) * HD] = result[
                        begin : begin + steps
                    ].astype(jnp.bfloat16)


def attend(packed, cache_keys, cache_values, lengths, heads, steps, keyval_real):
    chunks, G = packed.shape[0] - 1, packed.shape[1]
    query_rows = chunks * G * PACK
    cache_len = cache_keys.shape[0]
    span = 2048
    whole = pl.BlockSpec(packed.shape, lambda p: (0, 0, 0, 0))
    return pl.pallas_call(
        functools.partial(attend_kernel, (heads, steps, keyval_real)),
        grid=(cache_len // span,),
        out_shape=(
            jax.ShapeDtypeStruct((steps, heads * HD), jnp.bfloat16),
            jax.ShapeDtypeStruct((steps, 2 * HD), jnp.bfloat16),
        ),
        in_specs=[
            pl.BlockSpec(memory_space=pltpu.SMEM),
            whole,
            pl.BlockSpec((span, HD), lambda p: (p, 0)),
            pl.BlockSpec((span, HD), lambda p: (p, 0)),
        ],
        out_specs=(
            pl.BlockSpec((steps, heads * HD), lambda p: (0, 0)),
            pl.BlockSpec((steps, 2 * HD), lambda p: (0, 0)),
        ),
        scratch_shapes=[
            pltpu.VMEM((query_rows, HD), jnp.float32),
            pltpu.VMEM((query_rows, LANES), jnp.float32),
            pltpu.VMEM((query_rows, LANES), jnp.float32),
        ],
        compiler_params=pltpu.CompilerParams(vmem_limit_bytes=32 * 2**20),
        cost_estimate=pl.CostEstimate(
            flops=4 * query_rows * cache_len * HD,
            bytes_accessed=4 * cache_len * HD,
            transcendentals=query_rows * cache_len,
        ),
    )(lengths, packed, cache_keys, cache_values)


def on_device(tokens, norm_gain, w_query, w_keyval, cache_keys, cache_values, lengths):
    steps = tokens.shape[2]
    Y, Z = lax.axis_size("gy"), lax.axis_size("gz")
    heads = w_query.shape[1] * Y // HD
    keyval_real = w_keyval.shape[1] // Z
    missing = -keyval_real % LANES
    if missing:
        split = w_keyval.reshape(w_keyval.shape[0], Z, keyval_real)
        w_keyval = jnp.pad(split, ((0, 0), (0, 0), (0, missing))).reshape(w_keyval.shape[0], -1)
    packed = project(tokens, norm_gain, w_query, w_keyval)
    attended, entries = attend(
        packed, cache_keys[0, 0], cache_values[0, 0], lengths, heads, steps, keyval_real
    )
    return (attended[None, None], entries[None, None])


def solution(mesh):
    return jax.shard_map(
        on_device,
        mesh=mesh,
        in_specs=(
            P("gz", "gy", None, "gx"),
            P("gx"),
            P("gx", "gy"),
            P("gx", "gy"),
            P("gz", ("gx", "gy"), None, None),
            P("gz", ("gx", "gy"), None, None),
            P("gz", ("gx", "gy")),
        ),
        out_specs=(P("gz", ("gx", "gy"), None, None), P("gz", ("gx", "gy"), None, None)),
        check_vma=False,
    )
```

```python
import functools
import math

import jax
import jax.numpy as jnp
from jax import lax
from jax.experimental import pallas as pl
from jax.experimental.pallas import tpu as pltpu
from jax.sharding import PartitionSpec as P

D = 18432
HD = 256
OUTER = 4
LANES = 128
PACK = 16
AHEAD = 2
WIDTH = 1024
MESH = pl.DeviceIdType.MESH


def project_kernel(
    sizes,
    x_hbm,
    gain_hbm,
    wq_hbm,
    wkv_hbm,
    out_ref,
    x_ref,
    gain_ref,
    wq,
    wkv,
    raw,
    rows,
    stat_send,
    stat_recv,
    scale_send,
    scale_recv,
    product,
    a_send,
    a_recv,
    kept,
    b_send,
    b_recv,
    own,
    c_send,
    c_recv,
    w_sem,
    in_sem,
    st_ssem,
    st_rsem,
    sc_ssem,
    sc_rsem,
    y_ssem,
    y_rsem,
    k_ssem,
    k_rsem,
    a_ssem,
    a_rsem,
    b_ssem,
    b_rsem,
    c_ssem,
    c_rsem,
):
    X, Y, Z, seqs, steps = sizes
    NZ = OUTER
    NX = X // NZ
    G = Y * Z
    block = seqs * steps
    group = Y * steps
    per_block = seqs // Y
    dest_rows = Z * group
    query_half = wq.shape[1]
    keyval_half = wkv.shape[1]
    width = a_send.shape[-1]
    query_chunks = query_half // width
    chunks = query_chunks + 1
    packs = c_send.shape[0]
    subs = query_chunks // (packs - 1)

    i = lax.axis_index("gx")
    j = lax.axis_index("gy")
    k = lax.axis_index("gz")
    zi = i // NX
    xi = i % NX
    me = j * Z + k

    def chunk_width(c):
        return width if c < query_chunks else keyval_half

    def query_load(c):
        begin = pl.multiple_of(k * query_half + c * width, LANES)
        return pltpu.make_async_copy(
            wq_hbm.at[:, pl.ds(begin, width)],
            wq.at[:, pl.ds(c * width, width)],
            w_sem.at[c],
        )

    keyval_load = pltpu.make_async_copy(
        wkv_hbm.at[:, pl.ds(pl.multiple_of(k * keyval_half, LANES), keyval_half)],
        wkv,
        w_sem.at[query_chunks],
    )
    token_load = pltpu.make_async_copy(x_hbm, x_ref, in_sem.at[0])
    gain_load = pltpu.make_async_copy(gain_hbm, gain_ref, in_sem.at[1])
    token_load.start()
    gain_load.start()
    loads = [query_load(c) for c in range(query_chunks)] + [keyval_load]

    barrier = pltpu.get_barrier_semaphore()
    for d in range(1, X):
        pl.semaphore_signal(
            barrier, inc=1, device_id={"gx": (i + d) % X, "gy": j, "gz": k}, device_id_type=MESH
        )
    for dj in range(Y):
        for dk in range(Z):
            if dj or dk:
                pl.semaphore_signal(
                    barrier,
                    inc=1,
                    device_id={"gx": i, "gy": (j + dj) % Y, "gz": (k + dk) % Z},
                    device_id_type=MESH,
                )

    token_load.wait()
    values = jnp.concatenate(
        [x_ref[0, q].astype(jnp.float32) for q in range(seqs)], axis=0
    )

    def row_range(dj, dk):
        g = ((j + Y - dj) % Y) * Z + (k + Z - dk) % Z
        return pl.ds(pl.multiple_of(g * block, block), block)

    raw[row_range(0, 0), :] = values.astype(jnp.bfloat16)
    row_sum = jnp.sum(values, axis=1, keepdims=True)
    row_square = jnp.sum(values * values, axis=1, keepdims=True)
    lane = lax.broadcasted_iota(jnp.int32, (block, LANES), 1)
    packed = jnp.where(lane == 0, row_sum, jnp.where(lane == 1, row_square, 0.0))
    packed = jnp.concatenate(
        (packed, jnp.zeros((LANES - block, LANES), jnp.float32)), axis=0
    )
    stat_send[...] = packed.T[:8]

    pl.semaphore_wait(barrier, X - 1 + G - 1)

    sends = []

    def send(src, dst, ssem, rsem, di, dj, dk):
        copy = pltpu.make_async_remote_copy(
            src_ref=src,
            dst_ref=dst,
            send_sem=ssem,
            recv_sem=rsem,
            device_id={"gx": di, "gy": dj, "gz": dk},
            device_id_type=MESH,
        )
        copy.start()
        sends.append(copy)
        return copy

    stat_copies = [
        send(stat_send, stat_recv.at[d], st_ssem.at[d], st_rsem.at[d], (i + d) % X, j, k)
        for d in range(1, X)
    ]

    def raw_block(dj):
        return raw.at[row_range(dj, 0), :]

    y_copies = [None] + [
        send(raw_block(0), raw_block(0), y_ssem.at[dj], y_rsem.at[dj], i, (j + dj) % Y, k)
        for dj in range(1, Y)
    ]
    k_copies = {}

    def pass_on(dj):
        for dk in range(1, Z):
            k_copies[dj, dk] = send(
                raw_block(dj),
                raw_block(dj),
                k_ssem.at[dj, dk],
                k_rsem.at[dj, dk],
                i,
                j,
                (k + dk) % Z,
            )

    pass_on(0)
    for load in loads:
        load.start()
    total = stat_send[...]
    for d in range(1, X):
        stat_copies[d - 1].wait_recv()
        total = total + stat_recv[d]
    center = total[0:1] / D
    spread = total[1:2] / D - center * center
    scale_send[...] = jnp.concatenate(
        (center, lax.rsqrt(spread + 1e-05), jnp.zeros((6, LANES), jnp.float32)), axis=0
    )
    scale_copies = {}
    for dj in range(Y):
        for dk in range(Z):
            if dj or dk:
                slot = dj * Z + dk
                scale_copies[slot] = send(
                    scale_send,
                    scale_recv.at[slot],
                    sc_ssem.at[slot],
                    sc_rsem.at[slot],
                    i,
                    (j + dj) % Y,
                    (k + dk) % Z,
                )
    for dj in range(1, Y):
        y_copies[dj].wait_recv()
        pass_on(dj)
    for copy in scale_copies.values():
        copy.wait_recv()
    scales = [scale_send[...]] + [scale_recv[slot] for slot in range(1, G)]
    if 8 * G < LANES:
        scales.append(jnp.zeros((LANES - 8 * G, LANES), jnp.float32))
    scales = jnp.concatenate(scales, axis=0).T
    gain_load.wait()
    gain = gain_ref[...].reshape(1, gain_ref.shape[0])
    for dk in range(Z):
        for dj in range(Y):
            if dk:
                k_copies[dj, dk].wait_recv()
            here = row_range(dj, dk)
            slot = dj * Z + dk
            center = scales[:block, 8 * slot : 8 * slot + 1]
            factor = scales[:block, 8 * slot + 1 : 8 * slot + 2]
            rows[here, :] = (
                (raw[here, :].astype(jnp.float32) - center) * factor * gain
            ).astype(jnp.bfloat16)

    def multiply(c):
        loads[c].wait()
        if c < query_chunks:
            tile = HD

            def body(n, carry):
                here = pl.ds(pl.multiple_of(n * tile, tile), tile)
                there = pl.ds(pl.multiple_of(c * width + n * tile, tile), tile)
                product[:, here] = jnp.dot(
                    rows[...], wq[:, there], preferred_element_type=jnp.float32
                )
                return carry

            lax.fori_loop(0, width // tile, body, 0)
        else:
            product[:, :keyval_half] = jnp.dot(
                rows[...], wkv[...], preferred_element_type=jnp.float32
            )

    def rows_for(di, dk, w):
        g = (di // per_block) * Z + dk
        begin = pl.multiple_of(g * block + (di % per_block) * group, group)
        return product[pl.ds(begin, group), :w]

    a_copies = {}
    b_copies = {}
    c_copies = {}

    def stage_a(c):
        w = chunk_width(c)
        for dx in range(1, NX):
            to_x = (xi + dx) % NX
            for z in range(NZ):
                part = jnp.concatenate(
                    [rows_for(z * NX + to_x, dk, w) for dk in range(Z)], axis=0
                )
                a_send[c, dx, z * dest_rows : (z + 1) * dest_rows, :w] = part.astype(jnp.bfloat16)
            a_copies[c, dx] = send(
                a_send.at[c, dx, :, :w],
                a_recv.at[c, dx, :, :w],
                a_ssem.at[c, dx],
                a_rsem.at[c, dx],
                zi * NX + to_x,
                j,
                k,
            )
        for z in range(NZ):
            kept[c, z, :, :w] = jnp.concatenate(
                [rows_for(z * NX + xi, dk, w) for dk in range(Z)], axis=0
            )

    def stage_b(c):
        w = chunk_width(c)
        for dx in range(1, NX):
            a_copies[c, dx].wait_recv()
        for z in range(NZ):
            part = kept[c, z, :, :w]
            for dx in range(1, NX):
                part = part + a_recv[
                    c, dx, z * dest_rows : (z + 1) * dest_rows, :w
                ].astype(jnp.float32)
            kept[c, z, :, :w] = part
            b_send[c, z, :, :w] = part.astype(jnp.bfloat16)
        for dz in range(1, NZ):
            to_z = (zi + dz) % NZ
            b_copies[c, dz] = send(
                b_send.at[c, to_z, :, :w],
                b_recv.at[c, dz, :, :w],
                b_ssem.at[c, dz],
                b_rsem.at[c, dz],
                to_z * NX + xi,
                j,
                k,
            )
        own[c, :, :w] = kept[c, zi, :, :w]

    def stage_c(c):
        members = range(c * subs, (c + 1) * subs) if c < packs - 1 else [query_chunks]
        parts = []
        for m in members:
            w = chunk_width(m)
            part = own[m, :, :w]
            for dz in range(1, NZ):
                b_copies[m, dz].wait_recv()
                part = part + b_recv[m, dz, :, :w].astype(jnp.float32)
            parts.append(part)
        part = jnp.concatenate(parts, axis=1)
        w = part.shape[1]
        for dj in range(Y):
            for dk in range(Z):
                begin = (dk * Y + dj) * steps
                mine = part[begin : begin + steps, :]
                if w < HD:
                    mine = jnp.concatenate(
                        (mine, jnp.zeros((steps, HD - w), jnp.float32)), axis=1
                    )
                pieces = [mine[:, h * HD : (h + 1) * HD] for h in range(mine.shape[1] // HD)]
                missing = PACK - steps * len(pieces)
                if missing:
                    pieces.append(jnp.zeros((missing, HD), jnp.float32))
                c_send[c, dj * Z + dk] = jnp.concatenate(pieces, axis=0).astype(jnp.bfloat16)
        for dj in range(Y):
            for dk in range(Z):
                if dj or dk:
                    to_j = (j + dj) % Y
                    to_k = (k + dk) % Z
                    slot = dj * Z + dk
                    c_copies[c, slot] = send(
                        c_send.at[c, to_j * Z + to_k],
                        c_recv.at[c, me],
                        c_ssem.at[c, slot],
                        c_rsem.at[c, slot],
                        i,
                        to_j,
                        to_k,
                    )
        c_recv[c, me] = c_send[c, me]

    done = 0
    for c in range(chunks + AHEAD):
        if c < chunks:
            multiply(c)
            stage_a(c)
        if c >= AHEAD:
            stage_b(c - AHEAD)
            if done < packs - 1 and c - AHEAD >= (done + 1) * subs + 1:
                stage_c(done)
                done += 1
    for c in range(done, packs):
        stage_c(c)
    for copy in c_copies.values():
        copy.wait_recv()
    out_ref[...] = c_recv[...]
    for copy in sends:
        copy.wait_send()


def project(tokens, gain, w_query, w_keyval):
    X, Y, Z = lax.axis_size("gx"), lax.axis_size("gy"), lax.axis_size("gz")
    seqs, steps, depth = tokens.shape[1:]
    G = Y * Z
    NZ = OUTER
    NX = X // NZ
    block = seqs * steps
    dest_rows = Z * Y * steps
    query_half = w_query.shape[1] // Z
    keyval_half = w_keyval.shape[1] // Z
    pack_width = min(query_half, HD * (PACK // steps))
    width = WIDTH if pack_width % WIDTH == 0 else pack_width
    chunks = query_half // width + 1
    packs = query_half // pack_width + 1
    bf16, f32 = jnp.bfloat16, jnp.float32
    any_space = pl.BlockSpec(memory_space=pl.ANY)
    vmem = pl.BlockSpec(memory_space=pltpu.VMEM)
    dma = pltpu.SemaphoreType.DMA
    return pl.pallas_call(
        functools.partial(project_kernel, (X, Y, Z, seqs, steps)),
        out_shape=jax.ShapeDtypeStruct((packs, G, PACK, HD), bf16),
        in_specs=[any_space, any_space, any_space, any_space],
        out_specs=vmem,
        scratch_shapes=[
            pltpu.VMEM(tokens.shape, bf16),
            pltpu.VMEM(gain.shape, f32),
            pltpu.VMEM((depth, query_half), bf16),
            pltpu.VMEM((depth, keyval_half), bf16),
            pltpu.VMEM((G * block, depth), bf16),
            pltpu.VMEM((G * block, depth), bf16),
            pltpu.VMEM((8, LANES), f32),
            pltpu.VMEM((X, 8, LANES), f32),
            pltpu.VMEM((8, LANES), f32),
            pltpu.VMEM((G, 8, LANES), f32),
            pltpu.VMEM((G * block, width), f32),
            pltpu.VMEM((chunks, NX, NZ * dest_rows, width), bf16),
            pltpu.VMEM((chunks, NX, NZ * dest_rows, width), bf16),
            pltpu.VMEM((chunks, NZ, dest_rows, width), f32),
            pltpu.VMEM((chunks, NZ, dest_rows, width), bf16),
            pltpu.VMEM((chunks, NZ, dest_rows, width), bf16),
            pltpu.VMEM((chunks, dest_rows, width), f32),
            pltpu.VMEM((packs, G, PACK, HD), bf16),
            pltpu.VMEM((packs, G, PACK, HD), bf16),
            dma((chunks,)),
            dma((2,)),
            dma((X,)),
            dma((X,)),
            dma((G,)),
            dma((G,)),
            dma((Y,)),
            dma((Y,)),
            dma((Y, Z)),
            dma((Y, Z)),
            dma((chunks, NX)),
            dma((chunks, NX)),
            dma((chunks, NZ)),
            dma((chunks, NZ)),
            dma((packs, G)),
            dma((packs, G)),
        ],
        compiler_params=pltpu.CompilerParams(
            collective_id=0, has_side_effects=True, vmem_limit_bytes=55 * 2**20
        ),
        cost_estimate=pl.CostEstimate(
            flops=2 * G * block * depth * (query_half + keyval_half),
            bytes_accessed=2 * depth * (query_half + keyval_half),
            transcendentals=0,
        ),
    )(tokens, gain, w_query, w_keyval)


def attend_kernel(sizes, len_ref, q_ref, k_ref, v_ref, out_ref, new_ref, acc, top, total):
    heads, steps, keyval_real = sizes
    chunks, G = q_ref.shape[0] - 1, q_ref.shape[1]
    query_rows = chunks * G * PACK
    scale = HD**-0.5 * math.log2(math.e)
    p = pl.program_id(0)
    span = k_ref.shape[0]
    queries = q_ref[:chunks].reshape(query_rows, HD)
    transposed = (((1,), (1,)), ((), ()))

    @pl.when(p == 0)
    def _():
        entries = jnp.concatenate(
            [q_ref[chunks, g, :, :keyval_real] for g in range(G)], axis=1
        )
        new_ref[...] = entries[:steps]
        scores = scale * lax.dot_general(
            queries, entries[:, :HD], transposed, preferred_element_type=jnp.float32
        )
        row_step = lax.broadcasted_iota(jnp.int32, scores.shape, 0) % steps
        entry_step = lax.broadcasted_iota(jnp.int32, scores.shape, 1)
        scores = jnp.where(entry_step <= row_step, scores, -1e30)
        highest = jnp.max(scores, axis=1, keepdims=True)
        weights = jnp.exp2(scores - highest)
        top[...] = jnp.broadcast_to(highest, top.shape)
        total[...] = jnp.broadcast_to(jnp.sum(weights, axis=1, keepdims=True), total.shape)
        acc[...] = jnp.dot(
            weights.astype(jnp.bfloat16), entries[:, HD:], preferred_element_type=jnp.float32
        )

    def step(masked):
        scores = scale * lax.dot_general(
            queries, k_ref[...], transposed, preferred_element_type=jnp.float32
        )
        if masked:
            position = p * span + lax.broadcasted_iota(jnp.int32, (1, span), 1)
            scores = jnp.where(position < length, scores, -1e30)
        before = top[:, :1]
        highest = jnp.maximum(before, jnp.max(scores, axis=1, keepdims=True))
        weights = jnp.exp2(scores - highest)
        keep = jnp.exp2(before - highest)
        top[...] = jnp.broadcast_to(highest, top.shape)
        total[...] = total[...] * keep + jnp.sum(weights, axis=1, keepdims=True)
        acc[...] = acc[...] * keep + jnp.dot(
            weights.astype(jnp.bfloat16), v_ref[...], preferred_element_type=jnp.float32
        )

    length = len_ref[0, 0]
    begin, end = p * span, (p + 1) * span

    @pl.when(end <= length)
    def _():
        step(False)

    @pl.when((begin < length) & (length < end))
    def _():
        step(True)

    @pl.when(p == pl.num_programs(0) - 1)
    def _():
        result = acc[...] / total[:, :1]
        per_group = heads // G
        per_chunk = per_group // chunks
        for c in range(chunks):
            for g in range(G):
                for h in range(per_chunk):
                    begin = (c * G + g) * PACK + h * steps
                    head = g * per_group + c * per_chunk + h
                    out_ref[:, head * HD : (head + 1) * HD] = result[
                        begin : begin + steps
                    ].astype(jnp.bfloat16)


def attend(packed, cache_keys, cache_values, lengths, heads, steps, keyval_real):
    chunks, G = packed.shape[0] - 1, packed.shape[1]
    query_rows = chunks * G * PACK
    cache_len = cache_keys.shape[0]
    span = 4096
    whole = pl.BlockSpec(packed.shape, lambda p: (0, 0, 0, 0))
    return pl.pallas_call(
        functools.partial(attend_kernel, (heads, steps, keyval_real)),
        grid=(cache_len // span,),
        out_shape=(
            jax.ShapeDtypeStruct((steps, heads * HD), jnp.bfloat16),
            jax.ShapeDtypeStruct((steps, 2 * HD), jnp.bfloat16),
        ),
        in_specs=[
            pl.BlockSpec(memory_space=pltpu.SMEM),
            whole,
            pl.BlockSpec((span, HD), lambda p: (p, 0)),
            pl.BlockSpec((span, HD), lambda p: (p, 0)),
        ],
        out_specs=(
            pl.BlockSpec((steps, heads * HD), lambda p: (0, 0)),
            pl.BlockSpec((steps, 2 * HD), lambda p: (0, 0)),
        ),
        scratch_shapes=[
            pltpu.VMEM((query_rows, HD), jnp.float32),
            pltpu.VMEM((query_rows, LANES), jnp.float32),
            pltpu.VMEM((query_rows, LANES), jnp.float32),
        ],
        compiler_params=pltpu.CompilerParams(vmem_limit_bytes=32 * 2**20),
        cost_estimate=pl.CostEstimate(
            flops=4 * query_rows * cache_len * HD,
            bytes_accessed=4 * cache_len * HD,
            transcendentals=query_rows * cache_len,
        ),
    )(lengths, packed, cache_keys, cache_values)


def on_device(tokens, norm_gain, w_query, w_keyval, cache_keys, cache_values, lengths):
    steps = tokens.shape[2]
    Y, Z = lax.axis_size("gy"), lax.axis_size("gz")
    heads = w_query.shape[1] * Y // HD
    keyval_real = w_keyval.shape[1] // Z
    missing = -keyval_real % LANES
    if missing:
        split = w_keyval.reshape(w_keyval.shape[0], Z, keyval_real)
        w_keyval = jnp.pad(split, ((0, 0), (0, 0), (0, missing))).reshape(w_keyval.shape[0], -1)
    packed = project(tokens, norm_gain, w_query, w_keyval)
    attended, entries = attend(
        packed, cache_keys[0, 0], cache_values[0, 0], lengths, heads, steps, keyval_real
    )
    return (attended[None, None], entries[None, None])


def solution(mesh):
    return jax.shard_map(
        on_device,
        mesh=mesh,
        in_specs=(
            P("gz", "gy", None, "gx"),
            P("gx"),
            P("gx", "gy"),
            P("gx", "gy"),
            P("gz", ("gx", "gy"), None, None),
            P("gz", ("gx", "gy"), None, None),
            P("gz", ("gx", "gy")),
        ),
        out_specs=(P("gz", ("gx", "gy"), None, None), P("gz", ("gx", "gy"), None, None)),
        check_vma=False,
    )
```
